256 devices in a mesh: ep: 128 (over x, z_hi, y, core), dp: 2 (over z_lo).
Axes of the slice: x: 4, y: 4, z: 8 (z_hi: 4, z_lo: 2; z = z_hi * 2 + z_lo), core: 2. Of those that a mesh axis runs over, the one named last changes fastest.
Arguments:
- tokens: bfloat16 [32768, 2048], P(('ep', 'dp')), may hold values from -6 to 6
- out_grad: bfloat16 [32768, 2048], P(('ep', 'dp')), may hold values from -6 to 6
- routes: int32 [32768, 2], P(('ep', 'dp')), may hold values from 0 to 127, as said below
- gates: float32 [32768, 2], P(('ep', 'dp')), may hold values from 0.2 to 1
- hot_expert: int32 [1], replicated, may hold values from 0 to 127
- w_gate: bfloat16 [128, 768, 2048], P('ep', 'dp'), may hold values from -0.125 to 0.125
- w_up: bfloat16 [128, 768, 2048], P('ep', 'dp'), may hold values from -0.125 to 0.125
- w_down: bfloat16 [128, 768, 2048], P('ep', 'dp'), may hold values from -0.21875 to 0.21875
Outputs:
- layer_out: bfloat16 [32768, 2048], P(('ep', 'dp'))
- gate_grad: float32 [32768, 2], P(('ep', 'dp'))
- input_grad: bfloat16 [32768, 2048], P(('ep', 'dp'))
- grad_gate: bfloat16 [128, 768, 2048], P('ep', 'dp')
- grad_up: bfloat16 [128, 768, 2048], P('ep', 'dp')
- grad_down: bfloat16 [128, 768, 2048], P('ep', 'dp')
- hot_grads: bfloat16 [3, 2048, 768], P(None, 'ep', 'dp')
The draws below stay inside these ranges and needn't reach their ends.
Inputs may be any that keep to these rules, and one draw needn't show every extreme that they name: `routes`: every token has exactly one route with offset 0 (the hot expert) and one with an offset of 1 to 127. Within the 128 tokens of one device every offset of 1 to 127 is named at least once and at most twice, and one offset, which differs from device to device, is named exactly 2 times.
All inputs are finite; a program needn't handle non-finite values.
Results may differ from the reference program's by a relative error of at most 0.017.
Values may be sent and summed in bfloat16 or wider, within the bound.
No kernel may reach another device: no remote copies, remote signals or barrier semaphores. Data moves between devices by JAX's collectives and lax.ppermute only.
A program may use at most 192 MiB of HBM per device.

```python
import jax
import jax.numpy as jnp
from jax import lax

D = 2048
FF = 768
ROUTES = 2
TOK_DEV = 128
EXPERTS = 128
CAP = 2
TOKENS = 32768
N_EP = 128
N_DP = 2


def shuffled(key):
    return jax.random.permutation(key, EXPERTS - 1).astype(jnp.int32)


def draw_routes(key, part):
    key = jax.random.fold_in(key, 5)
    blocks = TOKENS // TOK_DEV
    others = EXPERTS - 1
    busiest = jax.random.randint(jax.random.fold_in(key, 12), (blocks, 1), 0, others, dtype=jnp.int32)
    order_keys = jax.random.split(jax.random.fold_in(key, 13), blocks * CAP)
    orders = jax.vmap(shuffled)(order_keys).reshape(blocks, CAP, others)
    final_order = orders[:, CAP - 1, :]
    leading = final_order[:, 0:1]
    swapped = jnp.where(final_order == busiest, leading, final_order)
    position = jnp.arange(others, dtype=jnp.int32)[None, :]
    swapped = jnp.where(position == 0, busiest, swapped)
    orders = jnp.concatenate([orders[:, :CAP - 1, :], swapped[:, None, :]], axis=1)
    listing = orders.reshape(blocks, CAP * others)[:, :TOK_DEV]
    chosen = listing + 1
    column = jax.random.randint(jax.random.fold_in(key, 14), (blocks, TOK_DEV), 0, 2, dtype=jnp.int32)
    hot_full = jnp.zeros((blocks, TOK_DEV), jnp.int32)
    left_route = jnp.where(column == 0, hot_full, chosen)
    right_route = jnp.where(column == 0, chosen, hot_full)
    return jnp.stack([left_route, right_route], axis=-1).reshape(TOKENS, ROUTES).astype(jnp.int32)


def level_of(own_key, shape, pieces, least, largest):
    factor_of, own = 1.0, jax.random.fold_in(own_key, 6)
    for axis_at, parts in pieces:
        draws = jnp.exp(jax.random.uniform(jax.random.fold_in(own, axis_at), (parts,), jnp.float32, least / len(pieces), largest / len(pieces)))
        factor_of = factor_of * jnp.repeat(draws, shape[axis_at] // parts).reshape([-1 if axis == axis_at else 1 for axis in range(len(shape))])
    return factor_of


def noise(stream_key, shape, deviation, reach, shards=(), kind=jnp.bfloat16):
    entries = jax.random.normal(stream_key, shape, jnp.float32) * deviation
    if len(shards) > 0:
        entries = level_of(stream_key, shape, shards, -0.22, 0.18) * entries
    return jnp.clip(entries, min=-reach, max=reach).astype(kind)


def setup_inputs(seed: int = 0) -> dict:
    keys = jax.random.split(jax.random.key(seed), 9)
    tokens = noise(keys[0], (TOKENS, D), 1.0, 6.0, ((0, 256),))
    out_grad = noise(keys[1], (TOKENS, D), 1.0, 6.0, ((0, 256),))
    routes = draw_routes(jax.random.fold_in(keys[8], 71), 0)
    gates = jnp.clip(0.2 + 0.8 * jax.random.uniform(keys[3], (TOKENS, ROUTES), jnp.float32) ** level_of(keys[3], (TOKENS, ROUTES), ((0, 256),), -0.2, 0.2), 0.2, 1.0)
    hot_expert = jax.random.randint(keys[4], (1,), 0, EXPERTS).astype(jnp.int32)
    w_gate = noise(keys[5], (EXPERTS, FF, D), D ** -0.5, 0.125, ((0, 128), (1, 2)))
    w_up = noise(keys[6], (EXPERTS, FF, D), D ** -0.5, 0.125, ((0, 128), (1, 2)))
    w_down = noise(keys[7], (EXPERTS, FF, D), FF ** -0.5, 0.21875, ((0, 128), (1, 2)))
    return dict(tokens=tokens, out_grad=out_grad, routes=routes, gates=gates, hot_expert=hot_expert, w_gate=w_gate, w_up=w_up, w_down=w_down)


def expert_pass(inputs, cotangents, gate_matrix, up_matrix, down_matrix):
    pre_gate = jnp.dot(inputs, gate_matrix.T, preferred_element_type=jnp.float32)
    pre_up = jnp.dot(inputs, up_matrix.T, preferred_element_type=jnp.float32)
    sigmoid_gate = jax.nn.sigmoid(pre_gate)
    hidden = (pre_gate * sigmoid_gate * pre_up).astype(jnp.bfloat16)
    expert_out = jnp.dot(hidden, down_matrix, preferred_element_type=jnp.float32).astype(jnp.bfloat16)
    back_hidden = jnp.dot(cotangents, down_matrix.T, preferred_element_type=jnp.float32)
    slope_term = sigmoid_gate * (1.0 + pre_gate * (1.0 - sigmoid_gate))
    back_gate = (back_hidden * pre_up * slope_term).astype(jnp.bfloat16)
    back_up = (back_hidden * pre_gate * sigmoid_gate).astype(jnp.bfloat16)
    back_input = (jnp.dot(back_gate, gate_matrix, preferred_element_type=jnp.float32)
                  + jnp.dot(back_up, up_matrix, preferred_element_type=jnp.float32)).astype(jnp.bfloat16)
    expert_out, back_input = lax.optimization_barrier((expert_out, back_input))
    grad_gate = jnp.dot(back_gate.T, inputs, preferred_element_type=jnp.float32)
    grad_up = jnp.dot(back_up.T, inputs, preferred_element_type=jnp.float32)
    grad_down = jnp.dot(hidden.T, cotangents, preferred_element_type=jnp.float32)
    return expert_out, back_input, grad_gate, grad_up, grad_down


def reference(tokens, out_grad, routes, gates, hot_expert, w_gate, w_up, w_down):
    hot_index = hot_expert[0]
    route_total = TOKENS * ROUTES
    hot_mask = routes == 0
    actual = ((routes + hot_index) % EXPERTS).astype(jnp.int32)
    flat_expert = jnp.where(hot_mask, EXPERTS, actual).reshape(-1).astype(jnp.int32)
    flat_token = (jnp.arange(route_total, dtype=jnp.int32) // ROUTES).astype(jnp.int32)
    flat_gate = gates.reshape(-1)
    ordering = jnp.argsort(flat_expert, stable=True).astype(jnp.int32)
    counts = jnp.sum((flat_expert[None, :] == jnp.arange(EXPERTS, dtype=jnp.int32)[:, None]).astype(jnp.int32), axis=1)
    starts = (jnp.cumsum(counts) - counts).astype(jnp.int32)
    window = CAP * N_EP * N_DP
    padded = jnp.concatenate([ordering, jnp.zeros((window,), jnp.int32)])
    offsets = jnp.arange(window, dtype=jnp.int32)
    pick_index = padded[starts[:, None] + offsets[None, :]]
    valid_mask = offsets[None, :] < counts[:, None]
    targets = jnp.where(valid_mask, pick_index, route_total).astype(jnp.int32)

    def one_expert(carried):
        expert_index, pick_row, valid_row = carried
        token_ids = flat_token[pick_row]
        inputs = jnp.where(valid_row[:, None], tokens[token_ids], jnp.zeros((), tokens.dtype))
        scaled = flat_gate[pick_row][:, None] * out_grad[token_ids].astype(jnp.float32)
        cotangents = jnp.where(valid_row[:, None], scaled, 0.0).astype(jnp.bfloat16)
        expert_out, back_input, grad_gate, grad_up, grad_down = expert_pass(
            inputs, cotangents, w_gate[expert_index], w_up[expert_index], w_down[expert_index])
        return (expert_out, back_input, grad_gate.astype(jnp.bfloat16),
                grad_up.astype(jnp.bfloat16), grad_down.astype(jnp.bfloat16))

    expert_outs, back_inputs, grad_gates, grad_ups, grad_downs = lax.map(
        one_expert, (jnp.arange(EXPERTS, dtype=jnp.int32), pick_index, valid_mask))
    flat_targets = targets.reshape(-1)
    route_out = jnp.zeros((route_total, D), expert_outs.dtype).at[flat_targets].set(
        expert_outs.reshape(-1, D), mode="drop")
    route_back = jnp.zeros((route_total, D), back_inputs.dtype).at[flat_targets].set(
        back_inputs.reshape(-1, D), mode="drop")

    hot_share = jnp.sum(jnp.where(hot_mask, gates, 0.0), axis=1)
    hot_cot = (hot_share[:, None] * out_grad.astype(jnp.float32)).astype(jnp.bfloat16)
    hot_out, hot_back, hot_gate, hot_up, hot_down = expert_pass(
        tokens, hot_cot, w_gate[hot_index], w_up[hot_index], w_down[hot_index])

    every_out = jnp.where(hot_mask[:, :, None], hot_out[:, None, :],
                          route_out.reshape(TOKENS, ROUTES, D)).astype(jnp.float32)
    layer_out = jnp.sum(gates[:, :, None] * every_out, axis=1).astype(jnp.bfloat16)
    gate_grad = jnp.sum(out_grad.astype(jnp.float32)[:, None, :] * every_out, axis=2)
    every_back = jnp.where(hot_mask[:, :, None], hot_back[:, None, :],
                           route_back.reshape(TOKENS, ROUTES, D)).astype(jnp.float32)
    input_grad = jnp.sum(every_back, axis=1).astype(jnp.bfloat16)
    hot_grads = jnp.stack([hot_gate.T, hot_up.T, hot_down.T], axis=0).astype(jnp.bfloat16)
    return layer_out, gate_grad, input_grad, grad_gates, grad_ups, grad_downs, hot_grads
```

```python
import jax
import jax.numpy as jnp
from jax import lax
from jax.sharding import Mesh
from jax.sharding import PartitionSpec as P

EP = ("x", "w", "y", "c")
F32 = jnp.float32
BF16 = jnp.bfloat16
LAST = (((1,), (1,)), ((), ()))
ROWS = (((0,), (0,)), ((), ()))


def shift(value, axis, step):
    size = lax.axis_size(axis)
    return lax.ppermute(value, axis, [(i, (i + step) % size) for i in range(size)])


def piece(value, dim, index, count):
    size = value.shape[dim] // count
    return lax.dynamic_slice_in_dim(value, index * size, size, dim)


def scatter_from(value, axis, dim, root):
    size, me = lax.axis_size(axis), lax.axis_index(axis)
    source = (me - root) % size
    result = piece(value, dim, me, size)
    for step in range(1, size):
        got = shift(piece(value, dim, (me + step) % size, size), axis, step)
        result = jnp.where(source == step, got, result)
    return result


def gather(value, axis, dim):
    size, me = lax.axis_size(axis), lax.axis_index(axis)
    length = value.shape[dim]
    shape = list(value.shape)
    shape[dim] = length * size
    got = [value, shift(value, axis, 1), shift(value, axis, -1)]
    out = jnp.zeros(shape, value.dtype)
    for step, part in ((0, got[0]), (1, got[1]), (-1, got[2])):
        out = lax.dynamic_update_slice_in_dim(out, part, ((me - step) % size) * length, dim)
    half = value.shape[0] // 2 // 8 * 8
    low = shift(got[1][:half], axis, 1)
    high = shift(got[2][half:], axis, -1)
    far = jnp.concatenate([low, high], axis=0)
    return lax.dynamic_update_slice_in_dim(out, far, ((me + 2) % size) * length, dim)


def reduce_to(value, axis, dim):
    size, me = lax.axis_size(axis), lax.axis_index(axis)
    total = piece(value, dim, me, size)
    for step in range(1, size):
        part = piece(value, dim, (me + step) % size, size).astype(BF16)
        total = total + shift(part, axis, step).astype(F32)
    return total


def hot_weights(own, hot_index):
    root = {"x": hot_index // 32, "w": hot_index // 8 % 4, "y": hot_index // 2 % 4}
    core, root_core = lax.axis_index("c"), hot_index % 2
    got = shift(piece(own, 0, 1 - core, 2), "c", 1)
    half = jnp.where(core == root_core, piece(own, 0, core, 2), got)
    middle = half.shape[0] // 2
    first, second = half[:middle], half[middle:]
    first = scatter_from(first, "x", 0, root["x"])
    second = scatter_from(second, "y", 0, root["y"])
    first = scatter_from(first, "y", 1, root["y"])
    second = scatter_from(second, "x", 1, root["x"])
    first = scatter_from(first, "w", 1, root["w"])
    second = scatter_from(second, "w", 1, root["w"])
    first, second = gather(first, "w", 1), gather(second, "w", 1)
    first, second = gather(first, "y", 1), gather(second, "x", 1)
    first, second = gather(first, "x", 0), gather(second, "y", 0)
    half = jnp.concatenate([first, second], axis=0)
    got = shift(half, "c", 1)
    low, high = jnp.where(core == 0, half, got), jnp.where(core == 0, got, half)
    return jnp.concatenate([low, high], axis=0)


def reduce_hot(total):
    rows, columns = total.shape
    core = lax.axis_index("c")
    block = rows // 128
    split = total.reshape(64, 2, block, columns)
    keep = lax.dynamic_slice_in_dim(split, core, 1, 1).reshape(64 * block, columns)
    send = lax.dynamic_slice_in_dim(split, 1 - core, 1, 1).reshape(64 * block, columns)
    keep = keep + shift(send.astype(BF16), "c", 1).astype(F32)
    cut = columns // 2 // 128 * 128
    first = keep[:, :cut].reshape(4, 4, 4, block, cut)
    second = keep[:, cut:].reshape(4, 4, 4, block, columns - cut)
    first, second = reduce_to(first, "x", 0), reduce_to(second, "y", 2)
    first, second = reduce_to(first, "y", 2), reduce_to(second, "x", 0)
    first, second = reduce_to(first, "w", 1), reduce_to(second, "w", 1)
    return jnp.concatenate([first.reshape(block, -1), second.reshape(block, -1)], axis=1)


def expert(inputs, cotangents, gate, up, down):
    pre_gate = lax.dot_general(inputs, gate, LAST, preferred_element_type=F32)
    pre_up = lax.dot_general(inputs, up, LAST, preferred_element_type=F32)
    back_hidden = lax.dot_general(cotangents, down, LAST, preferred_element_type=F32)
    sig = jax.nn.sigmoid(pre_gate)
    hidden = (pre_gate * sig * pre_up).astype(BF16)
    slope = sig * (1.0 + pre_gate * (1.0 - sig))
    back_gate = (back_hidden * pre_up * slope).astype(BF16)
    back_up = (back_hidden * pre_gate * sig).astype(BF16)
    out = jnp.dot(hidden, down, preferred_element_type=F32)
    dx = jnp.dot(back_gate, gate, preferred_element_type=F32) + jnp.dot(
        back_up, up, preferred_element_type=F32
    )
    return hidden, back_gate, back_up, out, dx


def swap_sum(parts, count):
    sent = jnp.concatenate([part[count:].astype(BF16) for part in parts], axis=0)
    got = shift(sent, "z", 1).astype(F32)
    return [part[:count] + got[i * count : (i + 1) * count] for i, part in enumerate(parts)]


def shards(tokens, out_grad, routes, gates, hot_expert, w_gate, w_up, w_down):
    experts = 128
    count, features = tokens.shape
    units = w_gate.shape[1]
    slots = 2 * experts
    hot_index = hot_expert[0]
    hot_mask = routes == 0
    hot_share = jnp.sum(jnp.where(hot_mask, gates, 0.0), axis=1)
    other_share = jnp.sum(jnp.where(hot_mask, 0.0, gates), axis=1)
    offset = jnp.sum(jnp.where(hot_mask, 0, routes), axis=1)
    target = (offset + hot_index) % experts
    order = jnp.arange(count, dtype=jnp.int32)
    earlier = (target[:, None] == target[None, :]) & (order[:, None] > order[None, :])
    rank = jnp.sum(earlier.astype(jnp.int32), axis=1)
    slot = target * 2 + rank
    lists = jnp.arange(slots, dtype=jnp.int32)
    place = (lists[:, None] == slot[None, :]).astype(BF16)

    grad_values = out_grad.astype(F32)
    other_cots = (other_share[:, None] * grad_values).astype(BF16)
    hot_cots = (hot_share[:, None] * grad_values).astype(BF16)

    packed = jnp.concatenate(
        [
            jnp.dot(place, values, preferred_element_type=F32).astype(BF16).reshape(experts, 2, features)
            for values in (tokens, other_cots)
        ],
        axis=1,
    )
    arrived = lax.all_to_all(packed, EP, split_axis=0, concat_axis=0, tiled=True)
    own_rows = arrived[:, :2].reshape(slots, features)
    own_cots = arrived[:, 2:].reshape(slots, features)

    own_weights = jnp.concatenate([w_gate[0], w_up[0], w_down[0]], axis=0)
    hot = hot_weights(own_weights, hot_index)
    hot_gate, hot_up, hot_down = hot[:units], hot[units : 2 * units], hot[2 * units :]

    pair_tokens = jnp.concatenate([tokens, shift(tokens, "z", 1)], axis=0)
    pair_hot_cots = jnp.concatenate([hot_cots, shift(hot_cots, "z", 1)], axis=0)
    pair_rows = jnp.concatenate([own_rows, shift(own_rows, "z", 1)], axis=0)
    pair_cots = jnp.concatenate([own_cots, shift(own_cots, "z", 1)], axis=0)

    hidden, back_gate, back_up, out, dx = expert(pair_rows, pair_cots, w_gate[0], w_up[0], w_down[0])
    own_out, own_dx = swap_sum([out, dx], slots)
    back = jnp.concatenate(
        [own_out.astype(BF16).reshape(experts, 2, features), own_dx.astype(BF16).reshape(experts, 2, features)],
        axis=1,
    )
    returned = lax.all_to_all(back, EP, split_axis=0, concat_axis=0, tiled=True)

    hot_hidden, hot_back_gate, hot_back_up, hot_part, hot_dx_part = expert(
        pair_tokens, pair_hot_cots, hot_gate, hot_up, hot_down
    )
    hot_out, hot_dx = swap_sum([hot_part, hot_dx_part], count)
    hot_grad = jnp.concatenate(
        [
            lax.dot_general(pair_tokens, hot_back_gate, ROWS, preferred_element_type=F32),
            lax.dot_general(pair_tokens, hot_back_up, ROWS, preferred_element_type=F32),
            lax.dot_general(pair_hot_cots, hot_hidden, ROWS, preferred_element_type=F32),
        ],
        axis=1,
    )
    hot_rows = reduce_hot(hot_grad).astype(BF16)
    hot_grads = hot_rows.reshape(hot_rows.shape[0], 3, units).transpose(1, 0, 2)

    own_gate_grad = lax.dot_general(back_gate, pair_rows, ROWS, preferred_element_type=F32)
    own_up_grad = lax.dot_general(back_up, pair_rows, ROWS, preferred_element_type=F32)
    own_down_grad = lax.dot_general(hidden, pair_cots, ROWS, preferred_element_type=F32)

    pick = (slot[:, None] == lists[None, :]).astype(BF16)
    other_out = jnp.dot(pick, returned[:, :2].reshape(slots, features), preferred_element_type=F32)
    other_dx = jnp.dot(pick, returned[:, 2:].reshape(slots, features), preferred_element_type=F32)
    hot_result = lax.optimization_barrier(hot_out.astype(BF16)).astype(F32)
    hot_dx_round = lax.optimization_barrier(hot_dx.astype(BF16)).astype(F32)
    layer_out = (other_share[:, None] * other_out + hot_share[:, None] * hot_result).astype(BF16)
    other_inner = jnp.sum(grad_values * other_out, axis=1)
    hot_inner = jnp.sum(grad_values * hot_result, axis=1)
    gate_grad = jnp.where(hot_mask, hot_inner[:, None], other_inner[:, None])
    input_grad = (other_dx + hot_dx_round).astype(BF16)
    return (
        layer_out,
        gate_grad,
        input_grad,
        own_gate_grad.astype(BF16)[None],
        own_up_grad.astype(BF16)[None],
        own_down_grad.astype(BF16)[None],
        hot_grads,
    )


def solution(mesh):
    fine = Mesh(mesh.devices.reshape(4, 4, 4, 2, 2), EP + ("z",))
    rows = P(EP + ("z",), None)
    weights = P(EP, "z", None)
    return jax.shard_map(
        shards,
        mesh=fine,
        in_specs=(rows, rows, rows, rows, P(), weights, weights, weights),
        out_specs=(rows, rows, rows, weights, weights, weights, P(None, EP, "z")),
        check_vma=False,
    )
```

```python
import jax
import jax.numpy as jnp
from jax import lax
from jax.sharding import Mesh
from jax.sharding import PartitionSpec as P

EP = ("x", "w", "y", "c")
F32 = jnp.float32
BF16 = jnp.bfloat16
LAST = (((1,), (1,)), ((), ()))
ROWS = (((0,), (0,)), ((), ()))


def shift(value, axis, step):
    size = lax.axis_size(axis)
    return lax.ppermute(value, axis, [(i, (i + step) % size) for i in range(size)])


def after(value, *others):
    for other in others:
        first = lax.slice(other, (0,) * other.ndim, (1,) * other.ndim).reshape(())
        value = jnp.where(first > jnp.inf, jnp.zeros_like(value), value)
    return value


def piece(value, dim, index, count):
    size = value.shape[dim] // count
    return lax.dynamic_slice_in_dim(value, index * size, size, dim)


def scatter_from(value, axis, dim, root):
    size, me = lax.axis_size(axis), lax.axis_index(axis)
    source = (me - root) % size
    result = piece(value, dim, me, size)
    for step in range(1, size):
        got = shift(piece(value, dim, (me + step) % size, size), axis, step)
        result = jnp.where(source == step, got, result)
    return result


def spread(value, axis, root):
    size, me = lax.axis_size(axis), lax.axis_index(axis)
    source = (me - root) % size
    result = value
    for step in range(1, size):
        result = jnp.where(source == step, shift(value, axis, step), result)
    return result


def gather(value, axis, dim):
    size, me = lax.axis_size(axis), lax.axis_index(axis)
    length = value.shape[dim]
    shape = list(value.shape)
    shape[dim] = length * size
    out = jnp.zeros(shape, value.dtype)
    for step in range(size):
        part = value if step == 0 else shift(value, axis, step)
        out = lax.dynamic_update_slice_in_dim(out, part, ((me - step) % size) * length, dim)
    return out


def reduce_to(value, axis, dim):
    size, me = lax.axis_size(axis), lax.axis_index(axis)
    total = piece(value, dim, me, size).astype(F32)
    for step in range(1, size):
        part = piece(value, dim, (me + step) % size, size)
        total = total + shift(part, axis, step).astype(F32)
    return total.astype(BF16)


def core_half(mats, hot_index):
    core = lax.axis_index("c")
    sent = jnp.concatenate([piece(m, 0, 1 - core, 2) for m in mats], axis=0)
    got = shift(sent, "c", 1)
    kept = jnp.concatenate([piece(m, 0, core, 2) for m in mats], axis=0)
    return jnp.where(core == hot_index % 2, kept, got)


def hot_pieces(half, hot_index):
    root = {"x": hot_index // 32, "w": hot_index // 8 % 4, "y": hot_index // 2 % 4}
    middle = half.shape[0] // 2
    first, second = half[:middle], half[middle:]
    first = scatter_from(first, "x", 0, root["x"])
    second = scatter_from(second, "y", 0, root["y"])
    first = scatter_from(first, "y", 1, root["y"])
    second = scatter_from(second, "x", 1, root["x"])
    rows = first.shape[0]
    both = spread(jnp.concatenate([first, second], axis=0), "w", root["w"])
    return gather(both[:rows], "y", 1), gather(both[rows:], "x", 1)


def place_rows(x, w, y, half):
    return half * 64 + (x * 16 + y * 4 + w if half == 0 else y * 16 + x * 4 + w)


def arrange(extra, order):
    rows = extra.reshape(4, 4, 4, 4, 4, -1).transpose(*order, 1, 3, 4, 5)
    return rows.reshape(4, 4, 4, 16, -1)


def reduce_hot(total, extra_out, extra_dx, early, late):
    rows, columns = total.shape
    block = rows // 128
    width = extra_out.shape[1] // 4
    parts = []
    for start, extra, order in ((0, extra_out, (0, 2)), (rows // 2, extra_dx, (2, 0))):
        lines = jnp.pad(arrange(extra, order), [(0, 0)] * 4 + [(0, columns - width)])
        sums = total[start : start + rows // 2].reshape(4, 4, 4, block, columns)
        parts.append(jnp.concatenate([sums, lines], axis=3))
    first, second = reduce_to(parts[0], "x", 0), reduce_to(parts[1], "y", 0)
    first, second = after(first, *early), after(second, *early)
    first, second = reduce_to(first, "y", 1), reduce_to(second, "x", 1)
    both = after(jnp.concatenate([first, second], axis=0), *late)
    both = reduce_to(both, "w", 2)[:, 0, 0]
    first, second = both[0, :block], both[1, :block]
    core, side = lax.axis_index("c"), lax.axis_index("z")
    extras = both[:, block:]
    sent = piece(extras, 1, 1 - core, 2).reshape(16, columns)
    got = shift(jnp.concatenate([jnp.where(core == 0, second, first), sent], axis=0), "c", 1)
    extras = piece(extras, 1, core, 2).astype(F32) + got[block:].reshape(2, 8, columns).astype(F32)
    got = got[:block]
    low = jnp.where(core == 0, first, got)
    high = jnp.where(core == 0, got, second)
    moves = []
    for x in range(4):
        for w in range(4):
            for y in range(4):
                for half in range(2):
                    moves.append((x * 32 + w * 8 + y * 2 + half, place_rows(x, w, y, half)))
    moved = lax.ppermute(jnp.stack([low, high], axis=1), EP, moves)
    extras = extras[:, :, :width]
    other = shift(piece(extras, 1, 1 - side, 2).astype(BF16).reshape(8, width), "z", 1)
    extras = piece(extras, 1, side, 2) + other.reshape(2, 4, width).astype(F32)
    return moved, extras.astype(BF16).reshape(2, 4 * width)


def activate(pre_gate, pre_up, back_hidden):
    sig = jax.nn.sigmoid(pre_gate)
    hidden = (pre_gate * sig * pre_up).astype(BF16)
    slope = sig * (1.0 + pre_gate * (1.0 - sig))
    back_gate = (back_hidden * pre_up * slope).astype(BF16)
    back_up = (back_hidden * pre_gate * sig).astype(BF16)
    return hidden, (back_gate, back_up)


def expert(inputs, cotangents, gate, up, down):
    pre_gate = lax.dot_general(inputs, gate, LAST, preferred_element_type=F32)
    pre_up = lax.dot_general(inputs, up, LAST, preferred_element_type=F32)
    back_hidden = lax.dot_general(cotangents, down, LAST, preferred_element_type=F32)
    hidden, (back_gate, back_up) = activate(pre_gate, pre_up, back_hidden)
    out = jnp.dot(hidden, down, preferred_element_type=F32)
    dx = jnp.dot(back_gate, gate, preferred_element_type=F32) + jnp.dot(
        back_up, up, preferred_element_type=F32
    )
    return hidden, back_gate, back_up, out, dx


def swap_sum(parts, count, axis):
    sent = jnp.concatenate([part[count:].astype(BF16) for part in parts], axis=0)
    got = shift(sent, axis, 1).astype(F32)
    return [part[:count] + got[i * count : (i + 1) * count] for i, part in enumerate(parts)]


def shards(tokens, out_grad, routes, gates, hot_expert, w_gate, w_up, w_down):
    experts = 128
    count, features = tokens.shape
    units = w_gate.shape[1]
    hot_index = hot_expert[0]
    hot_mask = routes == 0
    hot_share = jnp.sum(jnp.where(hot_mask, gates, 0.0), axis=1)
    other_share = jnp.sum(jnp.where(hot_mask, 0.0, gates), axis=1)
    offset = jnp.sum(jnp.where(hot_mask, 0, routes), axis=1)
    target = (offset + hot_index) % experts
    order = jnp.arange(count, dtype=jnp.int32)
    earlier = (target[:, None] == target[None, :]) & (order[:, None] > order[None, :])
    is_extra = jnp.any(earlier, axis=1)
    lists = jnp.arange(experts, dtype=jnp.int32)
    place = ((lists[:, None] == target[None, :]) & ~is_extra[None, :]).astype(BF16)

    grad_values = out_grad.astype(F32)
    other_cots = (other_share[:, None] * grad_values).astype(BF16)
    hot_cots = (hot_share[:, None] * grad_values).astype(BF16)

    side = lax.axis_index("z")
    chosen = is_extra[None, :].astype(BF16)
    extra_target = jnp.sum(jnp.where(is_extra, target, 0)).astype(BF16)
    extra = jnp.concatenate(
        [jnp.dot(chosen, v, preferred_element_type=F32).astype(BF16) for v in (tokens, other_cots)], axis=0
    ).reshape(4, features // 2)
    extra = jnp.concatenate([extra, jnp.full((4, 128), 1, BF16) * extra_target], axis=1)
    extra_other = shift(extra, "z", 1)
    extra = jnp.concatenate(
        [jnp.where(side == 0, extra, extra_other), jnp.where(side == 0, extra_other, extra)], axis=0
    )
    extras = lax.all_gather(extra, EP, axis=0, tiled=True).reshape(2 * experts, 2, 2, -1)

    half = core_half((w_gate[0], w_up[0], w_down[0]), hot_index)
    packed = jnp.stack(
        [jnp.dot(place, v, preferred_element_type=F32).astype(BF16) for v in (tokens, other_cots)], axis=1
    )
    arrived = lax.all_to_all(after(packed, half, extra), EP, split_axis=0, concat_axis=0, tiled=True)
    own = jnp.concatenate([arrived[:, 0], arrived[:, 1]], axis=0)
    other = shift(own, "z", 1)

    mine = after(jnp.stack([tokens, hot_cots], axis=0), own)
    pair = jnp.concatenate([mine, shift(mine, "z", 1)], axis=1)
    group = jnp.concatenate([pair, shift(pair, "c", 1)], axis=1)
    first, second = hot_pieces(half, hot_index)
    first = gather(after(first, own), "x", 0)

    me = lax.axis_index(EP)
    named = extras[:, 0, 0, features // 2 :][:, :1] == me.astype(BF16)
    extra_rows, extra_cots = [
        jnp.where(named, jnp.concatenate([extras[:, i, h, : features // 2] for h in range(2)], axis=1), 0)
        for i in range(2)
    ]
    pair_rows = jnp.concatenate([own[:experts], other[:experts], extra_rows], axis=0)
    pair_cots = jnp.concatenate([own[experts:], other[experts:], extra_cots], axis=0)

    hidden, back_gate, back_up, out, dx = expert(pair_rows, pair_cots, w_gate[0], w_up[0], w_down[0])
    pair = slice(experts, 2 * experts)
    sent = jnp.concatenate([out[pair].astype(BF16), dx[pair].astype(BF16)], axis=0)
    got = shift(sent, "z", 1).astype(F32)
    own_out, own_dx = out[:experts] + got[:experts], dx[:experts] + got[experts:]
    back = jnp.stack([own_out.astype(BF16), own_dx.astype(BF16)], axis=1)
    returned = lax.all_to_all(back, EP, split_axis=0, concat_axis=0, tiled=True)

    hot = jnp.concatenate([first, gather(after(second, sent), "y", 0)], axis=0)
    part = units // 2
    hot_in, hot_down = hot[: 2 * part], hot[2 * part :]
    pre = lax.dot_general(group[0], hot_in, LAST, preferred_element_type=F32)
    hot_hidden, hot_back = activate(
        pre[:, :part],
        pre[:, part:],
        lax.dot_general(group[1], hot_down, LAST, preferred_element_type=F32),
    )
    hot_back = jnp.concatenate(hot_back, axis=1)
    parts = [
        jnp.dot(hot_hidden, hot_down, preferred_element_type=F32),
        jnp.dot(hot_back, hot_in, preferred_element_type=F32),
    ]
    parts = swap_sum(parts, 2 * count, "c")
    z_sent = jnp.concatenate([p[count:].astype(BF16) for p in parts], axis=0)
    z_got = shift(z_sent, "z", 1)
    hot_out, hot_dx = [parts[i][:count] + z_got[i * count : (i + 1) * count].astype(F32) for i in range(2)]
    hot_grad = jnp.concatenate(
        [
            lax.dot_general(group[0], hot_back, ROWS, preferred_element_type=F32).astype(BF16),
            lax.dot_general(group[1], hot_hidden, ROWS, preferred_element_type=F32).astype(BF16),
        ],
        axis=1,
    )
    far = slice(2 * experts, 4 * experts)
    hot_rows, extra_sums = reduce_hot(after(hot_grad, back), out[far].astype(BF16), dx[far].astype(BF16), (z_sent,), (returned, z_got))
    hot_grads = hot_rows.reshape(-1, 2, 3, part).transpose(2, 0, 1, 3).reshape(3, -1, units)

    hidden, back_gate, back_up = [after(v, z_sent) for v in (hidden, back_gate, back_up)]
    own_gate_grad = lax.dot_general(back_gate, pair_rows, ROWS, preferred_element_type=F32)
    own_up_grad = lax.dot_general(back_up, pair_rows, ROWS, preferred_element_type=F32)
    own_down_grad = lax.dot_general(hidden, pair_cots, ROWS, preferred_element_type=F32)

    pick = (target[:, None] == lists[None, :]).astype(BF16)
    other_out, other_dx = [
        jnp.where(
            is_extra[:, None],
            extra_sums[i][None].astype(F32),
            jnp.dot(pick, returned[:, i], preferred_element_type=F32),
        )
        for i in range(2)
    ]
    hot_result = lax.optimization_barrier(hot_out.astype(BF16)).astype(F32)
    hot_dx_round = lax.optimization_barrier(hot_dx.astype(BF16)).astype(F32)
    layer_out = (other_share[:, None] * other_out + hot_share[:, None] * hot_result).astype(BF16)
    other_inner = jnp.sum(grad_values * other_out, axis=1)
    hot_inner = jnp.sum(grad_values * hot_result, axis=1)
    gate_grad = jnp.where(hot_mask, hot_inner[:, None], other_inner[:, None])
    input_grad = (other_dx + hot_dx_round).astype(BF16)
    return (
        layer_out,
        gate_grad,
        input_grad,
        own_gate_grad.astype(BF16)[None],
        own_up_grad.astype(BF16)[None],
        own_down_grad.astype(BF16)[None],
        hot_grads,
    )


def solution(mesh):
    fine = Mesh(mesh.devices.reshape(4, 4, 4, 2, 2), EP + ("z",))
    rows = P(EP + ("z",), None)
    weights = P(EP, "z", None)
    return jax.shard_map(
        shards,
        mesh=fine,
        in_specs=(rows, rows, rows, rows, P(), weights, weights, weights),
        out_specs=(rows, rows, rows, weights, weights, weights, P(None, EP, "z")),
        check_vma=False,
    )
```

```python
import jax
import jax.numpy as jnp
from jax import lax
from jax.sharding import Mesh
from jax.sharding import PartitionSpec as P

EP = ("x", "w", "y", "c")
F32 = jnp.float32
BF16 = jnp.bfloat16
LAST = (((1,), (1,)), ((), ()))
ROWS = (((0,), (0,)), ((), ()))


def shift(value, axis, step):
    size = lax.axis_size(axis)
    return lax.ppermute(value, axis, [(i, (i + step) % size) for i in range(size)])


def after(value, *others):
    for other in others:
        first = lax.slice(other, (0,) * other.ndim, (1,) * other.ndim).reshape(())
        value = jnp.where(first > jnp.inf, jnp.zeros_like(value), value)
    return value


def piece(value, dim, index, count):
    size = value.shape[dim] // count
    return lax.dynamic_slice_in_dim(value, index * size, size, dim)


def scatter_from(value, axis, dim, root):
    size, me = lax.axis_size(axis), lax.axis_index(axis)
    source = (me - root) % size
    result = piece(value, dim, me, size)
    for step in range(1, size):
        got = shift(piece(value, dim, (me + step) % size, size), axis, step)
        result = jnp.where(source == step, got, result)
    return result


def spread(value, axis, root):
    size, me = lax.axis_size(axis), lax.axis_index(axis)
    source = (me - root) % size
    result = value
    for step in range(1, size):
        result = jnp.where(source == step, shift(value, axis, step), result)
    return result


def gather(value, axis, dim):
    size, me = lax.axis_size(axis), lax.axis_index(axis)
    length = value.shape[dim]
    shape = list(value.shape)
    shape[dim] = length * size
    out = jnp.zeros(shape, value.dtype)
    for step in range(size):
        part = value if step == 0 else shift(value, axis, step)
        out = lax.dynamic_update_slice_in_dim(out, part, ((me - step) % size) * length, dim)
    return out


def reduce_to(value, axis, dim):
    size, me = lax.axis_size(axis), lax.axis_index(axis)
    total = piece(value, dim, me, size).astype(F32)
    for step in range(1, size):
        part = piece(value, dim, (me + step) % size, size)
        total = total + shift(part, axis, step).astype(F32)
    return total.astype(BF16)


def core_half(mats, hot_index):
    core = lax.axis_index("c")
    sent = jnp.concatenate([piece(m, 0, 1 - core, 2) for m in mats], axis=0)
    got = shift(sent, "c", 1)
    kept = jnp.concatenate([piece(m, 0, core, 2) for m in mats], axis=0)
    return jnp.where(core == hot_index % 2, kept, got)


def hot_pieces(half, hot_index, early):
    root = {"x": hot_index // 32, "w": hot_index // 8 % 4, "y": hot_index // 2 % 4}
    middle = half.shape[0] // 2
    first, second = half[:middle], half[middle:]
    first = scatter_from(first, "x", 0, root["x"])
    second = scatter_from(second, "y", 0, root["y"])
    first = scatter_from(first, "y", 1, root["y"])
    second = scatter_from(second, "x", 1, root["x"])
    rows = first.shape[0]
    both = after(jnp.concatenate([first, second], axis=0), early)
    both = spread(both, "w", root["w"])
    return gather(both[:rows], "y", 1), gather(both[rows:], "x", 1)


def place_rows(x, w, y, half):
    return half * 64 + (x * 16 + y * 4 + w if half == 0 else y * 16 + x * 4 + w)


def arrange(extra, order):
    rows = extra.reshape(4, 4, 4, 4, 4, -1).transpose(*order, 1, 3, 4, 5)
    return rows.reshape(4, 4, 4, 16, -1)


def reduce_hot(total, extra_out, extra_dx, early, late):
    rows, columns = total.shape
    block = rows // 128
    width = extra_out.shape[1] // 4
    parts = []
    for start, extra, order in ((0, extra_out, (0, 2)), (rows // 2, extra_dx, (2, 0))):
        lines = jnp.pad(arrange(extra, order), [(0, 0)] * 4 + [(0, columns - width)])
        sums = total[start : start + rows // 2].reshape(4, 4, 4, block, columns)
        parts.append(jnp.concatenate([sums, lines], axis=3))
    first, second = reduce_to(parts[0], "x", 0), reduce_to(parts[1], "y", 0)
    mark = second
    first, second = after(first, *early), after(second, *early)
    first, second = reduce_to(first, "y", 1), reduce_to(second, "x", 1)
    both = after(jnp.concatenate([first, second], axis=0), *late)
    both = reduce_to(both, "w", 2)[:, 0, 0]
    first, second = both[0, :block], both[1, :block]
    core, side = lax.axis_index("c"), lax.axis_index("z")
    extras = both[:, block:]
    sent = piece(extras, 1, 1 - core, 2).reshape(16, columns)
    got = shift(jnp.concatenate([jnp.where(core == 0, second, first), sent], axis=0), "c", 1)
    extras = piece(extras, 1, core, 2).astype(F32) + got[block:].reshape(2, 8, columns).astype(F32)
    got = got[:block]
    low = jnp.where(core == 0, first, got)
    high = jnp.where(core == 0, got, second)
    moves = []
    for x in range(4):
        for w in range(4):
            for y in range(4):
                for half in range(2):
                    moves.append((x * 32 + w * 8 + y * 2 + half, place_rows(x, w, y, half)))
    moved = lax.ppermute(jnp.stack([low, high], axis=1), EP, moves)
    extras = extras[:, :, :width]
    other = shift(piece(extras, 1, 1 - side, 2).astype(BF16).reshape(8, width), "z", 1)
    extras = piece(extras, 1, side, 2) + other.reshape(2, 4, width).astype(F32)
    return mark, moved, extras.astype(BF16).reshape(2, 4 * width)


def activate(pre_gate, pre_up, back_hidden):
    sig = jax.nn.sigmoid(pre_gate)
    hidden = (pre_gate * sig * pre_up).astype(BF16)
    slope = sig * (1.0 + pre_gate * (1.0 - sig))
    back_gate = (back_hidden * pre_up * slope).astype(BF16)
    back_up = (back_hidden * pre_gate * sig).astype(BF16)
    return hidden, (back_gate, back_up)


def expert(inputs, cotangents, gate, up, down):
    pre_gate = lax.dot_general(inputs, gate, LAST, preferred_element_type=F32)
    pre_up = lax.dot_general(inputs, up, LAST, preferred_element_type=F32)
    back_hidden = lax.dot_general(cotangents, down, LAST, preferred_element_type=F32)
    hidden, (back_gate, back_up) = activate(pre_gate, pre_up, back_hidden)
    out = jnp.dot(hidden, down, preferred_element_type=F32)
    dx = jnp.dot(back_gate, gate, preferred_element_type=F32) + jnp.dot(
        back_up, up, preferred_element_type=F32
    )
    return hidden, back_gate, back_up, out, dx


def swap_sum(parts, count, axis):
    sent = jnp.concatenate([part[count:].astype(BF16) for part in parts], axis=0)
    got = shift(sent, axis, 1).astype(F32)
    return [part[:count] + got[i * count : (i + 1) * count] for i, part in enumerate(parts)]


def shards(tokens, out_grad, routes, gates, hot_expert, w_gate, w_up, w_down):
    experts = 128
    count, features = tokens.shape
    units = w_gate.shape[1]
    hot_index = hot_expert[0]
    hot_mask = routes == 0
    hot_share = jnp.sum(jnp.where(hot_mask, gates, 0.0), axis=1)
    other_share = jnp.sum(jnp.where(hot_mask, 0.0, gates), axis=1)
    offset = jnp.sum(jnp.where(hot_mask, 0, routes), axis=1)
    target = (offset + hot_index) % experts
    order = jnp.arange(count, dtype=jnp.int32)
    earlier = (target[:, None] == target[None, :]) & (order[:, None] > order[None, :])
    is_extra = jnp.any(earlier, axis=1)
    lists = jnp.arange(experts, dtype=jnp.int32)
    place = ((lists[:, None] == target[None, :]) & ~is_extra[None, :]).astype(BF16)

    grad_values = out_grad.astype(F32)
    other_cots = (other_share[:, None] * grad_values).astype(BF16)
    hot_cots = (hot_share[:, None] * grad_values).astype(BF16)

    side = lax.axis_index("z")
    chosen = is_extra[None, :].astype(BF16)
    extra_target = jnp.sum(jnp.where(is_extra, target, 0)).astype(BF16)
    extra = jnp.concatenate(
        [jnp.dot(chosen, v, preferred_element_type=F32).astype(BF16) for v in (tokens, other_cots)], axis=0
    ).reshape(4, features // 2)
    extra = jnp.concatenate([extra, jnp.full((4, 128), 1, BF16) * extra_target], axis=1)
    extra_other = shift(extra, "z", 1)
    extra = jnp.concatenate(
        [jnp.where(side == 0, extra, extra_other), jnp.where(side == 0, extra_other, extra)], axis=0
    )
    extras = lax.all_gather(extra, EP, axis=0, tiled=True).reshape(2 * experts, 2, 2, -1)

    half = core_half((w_gate[0], w_up[0], w_down[0]), hot_index)
    packed = jnp.stack(
        [jnp.dot(place, v, preferred_element_type=F32).astype(BF16) for v in (tokens, other_cots)], axis=1
    )
    arrived = lax.all_to_all(after(packed, half, extra), EP, split_axis=0, concat_axis=0, tiled=True)
    own = jnp.concatenate([arrived[:, 0], arrived[:, 1]], axis=0)
    other = shift(own, "z", 1)

    mine = after(jnp.stack([tokens, hot_cots], axis=0), other)
    pair = jnp.concatenate([mine, shift(mine, "z", 1)], axis=1)
    group = jnp.concatenate([pair, shift(pair, "c", 1)], axis=1)
    first, second = hot_pieces(half, hot_index, own)
    first = gather(first, "x", 0)

    me = lax.axis_index(EP)
    named = extras[:, 0, 0, features // 2 :][:, :1] == me.astype(BF16)
    extra_rows, extra_cots = [
        jnp.where(named, jnp.concatenate([extras[:, i, h, : features // 2] for h in range(2)], axis=1), 0)
        for i in range(2)
    ]
    pair_rows = jnp.concatenate([own[:experts], other[:experts], extra_rows], axis=0)
    pair_cots = jnp.concatenate([own[experts:], other[experts:], extra_cots], axis=0)

    hidden, back_gate, back_up, out, dx = expert(pair_rows, pair_cots, w_gate[0], w_up[0], w_down[0])
    pair = slice(experts, 2 * experts)
    sent = jnp.concatenate([out[pair].astype(BF16), dx[pair].astype(BF16)], axis=0)
    got = shift(sent, "z", 1).astype(F32)
    own_out, own_dx = out[:experts] + got[:experts], dx[:experts] + got[experts:]
    back = jnp.stack([own_out.astype(BF16), own_dx.astype(BF16)], axis=1)
    returned = lax.all_to_all(back, EP, split_axis=0, concat_axis=0, tiled=True)

    hot = jnp.concatenate([first, gather(second, "y", 0)], axis=0)
    group = after(group, sent)
    part = units // 2
    hot_in, hot_down = hot[: 2 * part], hot[2 * part :]
    pre = lax.dot_general(group[0], hot_in, LAST, preferred_element_type=F32)
    hot_hidden, hot_back = activate(
        pre[:, :part],
        pre[:, part:],
        lax.dot_general(group[1], hot_down, LAST, preferred_element_type=F32),
    )
    hot_back = jnp.concatenate(hot_back, axis=1)
    parts = [
        jnp.dot(hot_hidden, hot_down, preferred_element_type=F32),
        jnp.dot(hot_back, hot_in, preferred_element_type=F32),
    ]
    parts = swap_sum(parts, 2 * count, "c")
    z_sent = jnp.concatenate([p[count:].astype(BF16) for p in parts], axis=0)
    z_got = shift(z_sent, "z", 1)
    hot_out, hot_dx = [parts[i][:count] + z_got[i * count : (i + 1) * count].astype(F32) for i in range(2)]
    hot_grad = jnp.concatenate(
        [
            lax.dot_general(group[0], hot_back, ROWS, preferred_element_type=F32).astype(BF16),
            lax.dot_general(group[1], hot_hidden, ROWS, preferred_element_type=F32).astype(BF16),
        ],
        axis=1,
    )
    far = slice(2 * experts, 4 * experts)
    mark, hot_rows, extra_sums = reduce_hot(hot_grad, out[far].astype(BF16), dx[far].astype(BF16), (back, z_sent), (returned, z_got))
    hot_grads = hot_rows.reshape(-1, 2, 3, part).transpose(2, 0, 1, 3).reshape(3, -1, units)

    hidden, back_gate, back_up = [after(v, mark) for v in (hidden, back_gate, back_up)]
    own_gate_grad = lax.dot_general(back_gate, pair_rows, ROWS, preferred_element_type=F32)
    own_up_grad = lax.dot_general(back_up, pair_rows, ROWS, preferred_element_type=F32)
    own_down_grad = lax.dot_general(hidden, pair_cots, ROWS, preferred_element_type=F32)

    pick = (target[:, None] == lists[None, :]).astype(BF16)
    other_out, other_dx = [
        jnp.where(
            is_extra[:, None],
            extra_sums[i][None].astype(F32),
            jnp.dot(pick, returned[:, i], preferred_element_type=F32),
        )
        for i in range(2)
    ]
    hot_result = lax.optimization_barrier(hot_out.astype(BF16)).astype(F32)
    hot_dx_round = lax.optimization_barrier(hot_dx.astype(BF16)).astype(F32)
    layer_out = (other_share[:, None] * other_out + hot_share[:, None] * hot_result).astype(BF16)
    other_inner = jnp.sum(grad_values * other_out, axis=1)
    hot_inner = jnp.sum(grad_values * hot_result, axis=1)
    gate_grad = jnp.where(hot_mask, hot_inner[:, None], other_inner[:, None])
    input_grad = (other_dx + hot_dx_round).astype(BF16)
    return (
        layer_out,
        gate_grad,
        input_grad,
        own_gate_grad.astype(BF16)[None],
        own_up_grad.astype(BF16)[None],
        own_down_grad.astype(BF16)[None],
        hot_grads,
    )


def solution(mesh):
    fine = Mesh(mesh.devices.reshape(4, 4, 4, 2, 2), EP + ("z",))
    rows = P(EP + ("z",), None)
    weights = P(EP, "z", None)
    return jax.shard_map(
        shards,
        mesh=fine,
        in_specs=(rows, rows, rows, rows, P(), weights, weights, weights),
        out_specs=(rows, rows, rows, weights, weights, weights, P(None, EP, "z")),
        check_vma=False,
    )
```
